256 devices in a mesh: gx: 64 (over z_lo, x, y, core), ba: 4 (over z_hi).
Axes of the slice: x: 4, y: 4, z: 8 (z_hi: 4, z_lo: 2; z = z_hi * 2 + z_lo), core: 2. Of those that a mesh axis runs over, the one named last changes fastest.
Arguments:
- spectra: bfloat16 [4, 2, 256, 20, 3456], P('ba', None, 'gx'), may hold values from -6 to 6
- cotangent: bfloat16 [4, 2, 256, 20, 3456], P('ba', None, 'gx'), may hold values from -6 to 6
- weights: bfloat16 [3456, 19200], P('gx'), may hold values from -1 to 1
Outputs:
- output_spectra: bfloat16 [4, 2, 256, 20, 3456], P('ba', None, 'gx')
- input_grad: bfloat16 [4, 2, 256, 20, 3456], P('ba', None, 'gx')
- weight_grad: float32 [3456, 19200], P('gx')
The draws below stay inside these ranges and needn't reach their ends.
All inputs are finite; a program needn't handle non-finite values.
Results may differ from the reference program's by a relative error of at most 0.0066.
Values may be sent and summed in bfloat16 or wider, within the bound.
A program may use at most 192 MiB of HBM per device.

```python
import math
import jax
import jax.numpy as jnp
from jax import lax

C = 20
X = 256
KX = 24
M = 3456
BATCH = 4


def block_scale(stream_key, shape, pieces, least, high):
    def one(position, blocks):
        draws = jax.random.uniform(jax.random.fold_in(jax.random.fold_in(stream_key, 6), position), (blocks,), jnp.float32, least / len(pieces), high / len(pieces))
        return jnp.repeat(jnp.exp(draws), shape[position] // blocks).reshape((-1,) + (1,) * (len(shape) - position - 1))

    factor_of = one(*pieces[0])
    for cut in pieces[1:]:
        factor_of = factor_of * one(*cut)
    return factor_of


def gaussian(own_key, extent, deviation, reach, shards=(), held_as=jnp.bfloat16):
    values = deviation * jax.random.normal(own_key, extent, jnp.float32)
    if shards:
        values = values * block_scale(own_key, extent, shards, -0.22, 0.18)
    return jnp.clip(values, -reach, reach).astype(held_as)


def setup_inputs(seed: int = 0) -> dict:
    seeds = jax.random.split(jax.random.key(seed), 4)
    return {
        "spectra": gaussian(seeds[0], (BATCH, 2, X, C, M), 1.0, 6.0, ((0, 4), (2, 64))),
        "cotangent": gaussian(seeds[1], (BATCH, 2, X, C, M), 1.0, 6.0, ((0, 4), (2, 64))),
        "weights": gaussian(seeds[2], (M, 2 * KX * C * C), (2 * C) ** -0.5, 1.0, ((0, 64),)),
    }


def build_table():
    mode_index = jnp.arange(KX, dtype=jnp.int32)
    wavenumber = jnp.where(mode_index < KX // 2, mode_index, mode_index - KX)
    positions = jnp.arange(X, dtype=jnp.int32)
    phases = wavenumber[:, None] * positions[None, :] % X
    angles = phases.astype(jnp.float32) * (2.0 * math.pi / X)
    factor = 1.0 / math.sqrt(X)
    cosine = jnp.cos(angles) * factor
    sine_part = jnp.sin(angles) * factor
    upper_rows = jnp.concatenate([cosine, sine_part], axis=1)
    lower_rows = jnp.concatenate([-sine_part, cosine], axis=1)
    return jnp.concatenate([upper_rows, lower_rows], axis=0).astype(jnp.bfloat16)

def transform(transform_rows, sample_field):
    flattened = sample_field.reshape(2 * X, -1)
    result = jnp.dot(transform_rows, flattened, preferred_element_type=jnp.float32)
    return result.reshape(2, KX, sample_field.shape[2], sample_field.shape[3]).astype(jnp.bfloat16)

def invert(transform_rows, modes):
    flattened = modes.reshape(2 * KX, -1)
    result = jnp.dot(transform_rows.T, flattened, preferred_element_type=jnp.float32)
    return result.reshape(2, X, modes.shape[2], modes.shape[3]).astype(jnp.bfloat16)

def contract(coeffs, weight_full):
    values = coeffs.astype(jnp.float32)
    real_part = jnp.einsum('kim,kiom->kom', values[0], weight_full[0]) - jnp.einsum('kim,kiom->kom', values[1], weight_full[1])
    imag_part = jnp.einsum('kim,kiom->kom', values[0], weight_full[1]) + jnp.einsum('kim,kiom->kom', values[1], weight_full[0])
    return jnp.stack([real_part, imag_part])

def adjoint(grad_modes, weight_full):
    values = grad_modes.astype(jnp.float32)
    real_part = jnp.einsum('kom,kiom->kim', values[0], weight_full[0]) + jnp.einsum('kom,kiom->kim', values[1], weight_full[1])
    imag_part = jnp.einsum('kom,kiom->kim', values[1], weight_full[0]) - jnp.einsum('kom,kiom->kim', values[0], weight_full[1])
    return jnp.stack([real_part, imag_part])

def outer_sum(coeffs, grad_modes):
    first = coeffs.astype(jnp.float32)
    second = grad_modes.astype(jnp.float32)
    real_part = jnp.einsum('kim,kom->kiom', first[0], second[0]) + jnp.einsum('kim,kom->kiom', first[1], second[1])
    imag_part = jnp.einsum('kim,kom->kiom', first[0], second[1]) - jnp.einsum('kim,kom->kiom', first[1], second[0])
    return jnp.stack([real_part, imag_part])

def reference(spectra, cotangent, weights):
    transform_rows = build_table()
    weight_full = weights.astype(jnp.float32).reshape(M, 2, KX, C, C).transpose(1, 2, 3, 4, 0)

    def sample(running, inputs_pair):
        sample_field, sample_grad = inputs_pair
        coeffs = transform(transform_rows, sample_field)
        mixed_modes = contract(coeffs, weight_full).astype(jnp.bfloat16)
        output = invert(transform_rows, mixed_modes)
        grad_modes = transform(transform_rows, sample_grad)
        back_modes = adjoint(grad_modes, weight_full).astype(jnp.bfloat16)
        grad_in = invert(transform_rows, back_modes)
        return (running + outer_sum(coeffs, grad_modes), (output, grad_in))
    initial = jnp.zeros((2, KX, C, C, M), jnp.float32)
    summed, (output_spectra, input_grad) = lax.scan(sample, initial, (spectra, cotangent))
    weight_grad = summed.transpose(4, 0, 1, 2, 3).reshape(M, 2 * KX * C * C)
    return (output_spectra, input_grad, weight_grad)
```

```python
import functools
import math

import jax
import jax.numpy as jnp
import numpy as np
from jax import lax
from jax.experimental import pallas as pl
from jax.experimental.pallas import tpu as pltpu
from jax.sharding import PartitionSpec as P

C = 20
X = 256
KX = 24
SHARD = 54
MODES = 3456
TILES = MODES // 128
PLANE = 32
COLS = 1152
NT = COLS // 128
GROUP = 8
GN = GROUP * C * C
CHUNK = 640
MESH = pl.DeviceIdType.MESH


def table():
    mode = np.arange(KX)
    wave = np.where(mode < KX // 2, mode, mode - KX)
    phases = wave[:, None] * np.arange(X)[None, :] % X
    angles = phases.astype(np.float32) * np.float32(2.0 * math.pi / X)
    factor = np.float32(1.0 / math.sqrt(X))
    c = np.cos(angles) * factor
    s = np.sin(angles) * factor
    full = np.concatenate([np.concatenate([c, s], 1), np.concatenate([-s, c], 1)], 0)
    return full.astype(jnp.bfloat16).astype(np.float32)


@functools.cache
def constants():
    f = table().reshape(2, 3, GROUP, 2, 2, PLANE, 4)
    f = f.transpose(4, 1, 0, 2, 5, 3, 6)
    fb = np.zeros((2, 2, 48, PLANE, 2, 8), np.float32)
    for z in range(2):
        rows = f[z].reshape(48, PLANE, 8)
        fb[z, 0, :, :, z] = rows
        fb[z, 1, :, :, 1 - z] = rows
    fb = fb.reshape(2, 96, 512)
    n = np.arange(GN)
    kk, i, o = n // (C * C), n // C % C, n % C
    r = np.arange(C * GROUP)
    ei = ((r // GROUP)[:, None] == i[None]) & ((r % GROUP)[:, None] == kk[None])
    eo = ((r // GROUP)[:, None] == o[None]) & ((r % GROUP)[:, None] == kk[None])
    bf = lambda a: a.astype(jnp.bfloat16)
    return bf(fb), bf(fb.transpose(0, 2, 1)), bf(ei.astype(np.float32)), bf(eo.astype(np.float32))


def spot(c):
    return 54 * c // 128, 54 * c % 128


def kernel(
    x_hbm, ct_hbm, w_hbm, fb_hbm, fbt_hbm, ei_hbm, eo_hbm,
    out_hbm, gin_hbm, wg_hbm,
    xb, xf, w, fb, fbt, ei, eo, sbuf, rbuf, zs, zr, coef, lown, lall, bt, mm, wg, ob,
    load_sem, ssem, rsem, zssem, zrsem, bssem, brsem, out_sem,
):
    me = lax.axis_index("gx")
    ba = lax.axis_index("ba")
    z = me // PLANE
    q = me % PLANE
    qx, qy, qc = q // 8, q // 2 % 4, q % 2

    def peer(j):
        dest = (qx + j // 8) % 4 * 8 + (qy + j // 2 % 4) % 4 * 2 + (qc + j % 2) % 2
        return dest

    def load(i, src, dst):
        copy = pltpu.make_async_copy(src, dst, load_sem.at[i])
        copy.start()
        return copy

    loads = [
        load(0, x_hbm, xb.at[0]),
        load(1, ct_hbm, xb.at[1]),
        load(2, fb_hbm, fb),
        load(3, ei_hbm, ei),
        load(4, eo_hbm, eo),
        load(5, w_hbm, w),
        load(6, fbt_hbm, fbt),
    ]

    bar = pltpu.get_barrier_semaphore()

    def greet(j, carry):
        pl.semaphore_signal(bar, inc=1, device_id=(z * PLANE + peer(j), ba), device_id_type=MESH)
        return carry

    lax.fori_loop(1, PLANE, greet, 0)
    zpeer = ((1 - z) * PLANE + q, ba)
    pl.semaphore_signal(bar, inc=1, device_id=zpeer, device_id_type=MESH)
    for d in range(1, 4):
        pl.semaphore_signal(bar, inc=1, device_id=(me, (ba + d) % 4), device_id_type=MESH)

    lane = lax.broadcasted_iota(jnp.int32, (8, 128), 1)

    def widen(which):
        def tile(t, carry):
            cols = pl.ds(pl.multiple_of(t * 128, 128), 128)
            for r in range(8):
                xf[t, r * 24 : r * 24 + C, :] = xb[which, r, :, cols].astype(jnp.float32)
            return carry

        lax.fori_loop(0, TILES, tile, 0)

    def pack(dest, store):
        halves = []
        for h in range(2):
            lane0 = 54 * (PLANE * h + dest)
            t0 = lane0 // 128
            amt = lane0 % 128
            t1 = jnp.minimum(t0 + 1, TILES - 1)
            mask = lane >= amt
            tiles = [None] * NT
            for c in range(C):
                T, pos = spot(c)
                a = xf[t0, pl.ds(c, 8, stride=24), :]
                b = xf[t1, pl.ds(c, 8, stride=24), :]
                v = pltpu.roll(jnp.where(mask, a, b), (pos + 128 - amt) % 128, 1)
                tiles[T] = v if pos == 0 else jnp.where(lane >= pos, v, tiles[T])
                if pos + 54 > 128:
                    tiles[T + 1] = v
            halves.append(tiles)
        for T in range(NT):
            both = jnp.concatenate([halves[0][T], halves[1][T]], axis=0)
            store(T, both.astype(jnp.bfloat16))

    def send(phase, dest):
        pltpu.make_async_remote_copy(
            src_ref=sbuf.at[phase, dest],
            dst_ref=rbuf.at[phase, q],
            send_sem=ssem.at[phase],
            recv_sem=rsem.at[phase],
            device_id=(z * PLANE + dest, ba),
            device_id_type=MESH,
        ).start()

    def received(phase):
        part = rbuf.at[phase, pl.ds(0, PLANE - 1)]
        pltpu.make_async_copy(part, part, rsem.at[phase]).wait()

    def scatter(phase):
        def own(T, value):
            rbuf[phase, q, :, T * 128 : T * 128 + 128] = value

        pack(q, own)

        def step(j, carry):
            dest = peer(j)

            def put(T, value):
                sbuf[phase, dest, :, T * 128 : T * 128 + 128] = value

            pack(dest, put)
            send(phase, dest)
            return carry

        lax.fori_loop(1, PLANE, step, 0)

    def swap(slot):
        copy = pltpu.make_async_remote_copy(
            src_ref=zs.at[slot], dst_ref=zr.at[slot], send_sem=zssem.at[slot],
            recv_sem=zrsem.at[slot], device_id=zpeer, device_id_type=MESH,
        )
        copy.start()
        return copy

    def transform(phase):
        rows = rbuf[phase].reshape(512, COLS)
        part = jnp.dot(fb[z, 48:96], rows, preferred_element_type=jnp.float32)
        zs[phase] = part.astype(jnp.bfloat16)
        copy = swap(phase)
        mine = jnp.dot(fb[z, 0:48], rows, preferred_element_type=jnp.float32)
        copy.wait_recv()
        coef[phase, ba] = (mine + zr[phase].astype(jnp.float32)).astype(jnp.bfloat16)
        return copy

    def gather(phase):
        copies = []
        for d in range(1, 4):
            copy = pltpu.make_async_remote_copy(
                src_ref=coef.at[phase, ba], dst_ref=coef.at[phase, ba],
                send_sem=bssem.at[phase], recv_sem=brsem.at[phase],
                device_id=(me, (ba + d) % 4), device_id_type=MESH,
            )
            copy.start()

    def gathered(phase):
        part = coef.at[phase, pl.ds(0, 3)]
        pltpu.make_async_copy(part, part, brsem.at[phase]).wait()
        pltpu.make_async_copy(part, part, bssem.at[phase]).wait()

    def turn(phase, sample, put):
        for pair in range(3):
            tiles = [
                coef[phase, sample, 16 * pair : 16 * pair + 16, T * 128 : T * 128 + 128].astype(
                    jnp.float32
                )
                for T in range(NT)
            ]
            for p in range(2):
                for c in range(C):
                    T, pos = spot(c)
                    v = tiles[T][8 * p : 8 * p + 8]
                    if pos + 54 > 128:
                        v = jnp.where(lane >= pos, v, tiles[T + 1][8 * p : 8 * p + 8])
                    if pos:
                        v = pltpu.roll(v, 128 - pos, 1)
                    bt[8 * c : 8 * c + 8, :] = v
                put(pair, p, bt[...].T[0:64, :].astype(jnp.bfloat16))

    def mix(phase, slot):
        def put(g, p, value):
            lown[g, 64 * p : 64 * p + 64, :] = value

        turn(phase, ba, put)
        expand, reduce = (ei, eo) if phase == 0 else (eo, ei)
        sign = -1.0 if phase == 0 else 1.0
        for g in range(3):

            def chunk(j, total):
                n0 = pl.multiple_of(j * CHUNK, 128)
                cols = pl.ds(n0, CHUNK)
                wide = jnp.dot(lown[g], expand[:, cols], preferred_element_type=jnp.float32)
                ar, ai = wide[0:54], wide[64:118]
                wr = w[:, pl.ds(pl.multiple_of(n0 + g * GN, 128), CHUNK)].astype(jnp.float32)
                wi = w[:, pl.ds(pl.multiple_of(n0 + g * GN + 3 * GN, 128), CHUNK)].astype(
                    jnp.float32
                )
                if phase == 0:
                    tr, ti = ar * wr - ai * wi, ar * wi + ai * wr
                else:
                    tr, ti = wr * ar + wi * ai, wr * ai - wi * ar
                zero = jnp.zeros((10, CHUNK), jnp.float32)
                both = jnp.concatenate([tr, zero, ti, zero], axis=0).astype(jnp.bfloat16)
                return total + lax.dot_general(
                    both, reduce[:, cols], (((1,), (1,)), ((), ())),
                    preferred_element_type=jnp.float32,
                )

            mm[g] = lax.fori_loop(
                0, GN // CHUNK, chunk, jnp.zeros((128, C * GROUP), jnp.float32)
            )
            back = mm[g].T
            bt[...] = back
            halves = []
            for p in range(2):
                tiles = [None] * NT
                for c in range(C):
                    T, pos = spot(c)
                    v = bt[8 * c : 8 * c + 8, :]
                    shift = (pos + 64 * p) % 128
                    if shift:
                        v = pltpu.roll(v, shift, 1)
                    tiles[T] = v if pos == 0 else jnp.where(lane >= pos, v, tiles[T])
                    if pos + 54 > 128:
                        tiles[T + 1] = v
                halves.append(tiles)
            for T in range(NT):
                both = jnp.concatenate([halves[0][T], halves[1][T]], axis=0)
                zs[slot, 16 * g : 16 * g + 16, T * 128 : T * 128 + 128] = both.astype(jnp.bfloat16)
        return swap(slot)

    def invert(phase, slot, copy):
        copy.wait_recv()
        modes = jnp.concatenate([zs[slot], zr[slot]], axis=0)
        step = 128
        for b in range(512 // step):
            rows = jnp.dot(
                fbt[z, b * step : b * step + step, :], modes, preferred_element_type=jnp.float32
            )
            first = b * step // 16
            sbuf[phase, first : first + step // 16] = rows.astype(jnp.bfloat16).reshape(
                step // 16, 16, COLS
            )
        rbuf[phase, q] = sbuf[phase, q]

        def one(j, carry):
            send(phase, peer(j))
            return carry

        lax.fori_loop(1, PLANE, one, 0)

    def unpack(phase, slot, dst):
        for h in range(2):

            def one(source, carry):
                lane0 = 54 * (PLANE * h + source)
                t0 = lane0 // 128
                amt = lane0 % 128
                mask = lane >= amt
                tiles = [
                    rbuf[phase, source, :, T * 128 : T * 128 + 128].astype(jnp.float32)[
                        8 * h : 8 * h + 8
                    ]
                    for T in range(NT)
                ]
                for c in range(C):
                    T, pos = spot(c)
                    v = tiles[T]
                    if pos + 54 > 128:
                        v = jnp.where(lane >= pos, v, tiles[T + 1])
                    v = pltpu.roll(v, (amt + 128 - pos) % 128, 1)
                    rows = pl.ds(c, 8, stride=24)
                    xf[t0, rows, :] = jnp.where(mask, v, xf[t0, rows, :])
                    xf[t0 + 1, rows, :] = v
                return carry

            lax.fori_loop(0, PLANE, one, 0)

        def tile(t, carry):
            cols = pl.ds(pl.multiple_of(t * 128, 128), 128)
            for r in range(8):
                ob[slot, r, :, cols] = xf[t, r * 24 : r * 24 + C, :].astype(jnp.bfloat16)
            return carry

        lax.fori_loop(0, TILES, tile, 0)
        copy = pltpu.make_async_copy(ob.at[slot], dst, out_sem.at[slot])
        copy.start()
        return copy

    def outer():
        for phase in range(2):

            def sample(s, carry):
                def put(g, p, value):
                    lall[phase, g, pl.ds(pl.multiple_of(p * 256 + s * 64, 64), 64), :] = value

                turn(phase, s, put)
                return carry

            lax.fori_loop(0, 4, sample, 0)
        for g in range(3):

            def chunk(j, carry):
                n0 = pl.multiple_of(j * CHUNK, 128)
                cols = pl.ds(n0, CHUNK)
                a = jnp.dot(lall[0, g], ei[:, cols], preferred_element_type=jnp.float32)
                b = jnp.dot(lall[1, g], eo[:, cols], preferred_element_type=jnp.float32)
                re = im = None
                for s in range(4):
                    ar, ai = a[64 * s : 64 * s + 54], a[256 + 64 * s : 256 + 64 * s + 54]
                    br, bi = b[64 * s : 64 * s + 54], b[256 + 64 * s : 256 + 64 * s + 54]
                    r, i = ar * br + ai * bi, ar * bi - ai * br
                    re, im = (r, i) if s == 0 else (re + r, im + i)
                wg[:, pl.ds(pl.multiple_of(n0 + g * GN, 128), CHUNK)] = re
                wg[:, pl.ds(pl.multiple_of(n0 + g * GN + 3 * GN, 128), CHUNK)] = im
                return carry

            lax.fori_loop(0, GN // CHUNK, chunk, 0)
        copy = pltpu.make_async_copy(wg, wg_hbm, out_sem.at[2])
        copy.start()
        return copy

    loads[0].wait()
    widen(0)
    pl.semaphore_wait(bar, PLANE - 1 + 1 + 3)
    scatter(0)
    loads[1].wait()
    widen(1)
    scatter(1)
    for copy in loads[2:]:
        copy.wait()
    swaps = []
    received(0)
    swaps.append(transform(0))
    swaps.append(mix(0, 2))
    gather(0)
    invert(2, 2, swaps[-1])
    received(1)
    swaps.append(transform(1))
    swaps.append(mix(1, 3))
    gather(1)
    invert(3, 3, swaps[-1])
    received(2)
    done = [unpack(2, 0, out_hbm)]
    gathered(0)
    gathered(1)
    done.append(outer())
    received(3)
    done.append(unpack(3, 1, gin_hbm))
    for copy in swaps:
        copy.wait_send()
    for phase in range(4):
        part = sbuf.at[phase, pl.ds(0, PLANE - 1)]
        pltpu.make_async_copy(part, part, ssem.at[phase]).wait()
    for copy in done:
        copy.wait()


def on_device(spectra, cotangent, weights):
    fb, fbt, ei, eo = constants()
    bf, f32 = jnp.bfloat16, jnp.float32
    vm = pltpu.VMEM
    dma = pltpu.SemaphoreType.DMA
    out, gin, wg = pl.pallas_call(
        kernel,
        out_shape=[
            jax.ShapeDtypeStruct((8, C, MODES), bf),
            jax.ShapeDtypeStruct((8, C, MODES), bf),
            jax.ShapeDtypeStruct((SHARD, 6 * GN), f32),
        ],
        in_specs=[pl.BlockSpec(memory_space=pl.ANY)] * 7,
        out_specs=[pl.BlockSpec(memory_space=pl.ANY)] * 3,
        scratch_shapes=[
            vm((2, 8, C, MODES), bf),
            vm((TILES + 1, 192, 128), f32),
            vm((SHARD, 6 * GN), bf),
            vm((2, 96, 512), bf),
            vm((2, 512, 96), bf),
            vm((C * GROUP, GN), bf),
            vm((C * GROUP, GN), bf),
            vm((4, PLANE, 16, COLS), bf),
            vm((4, PLANE, 16, COLS), bf),
            vm((4, 48, COLS), bf),
            vm((4, 48, COLS), bf),
            vm((2, 4, 48, COLS), bf),
            vm((3, 128, C * GROUP), bf),
            vm((2, 3, 512, C * GROUP), bf),
            vm((C * GROUP, 128), f32),
            vm((3, 128, C * GROUP), f32),
            vm((SHARD, 6 * GN), f32),
            vm((2, 8, C, MODES), bf),
            dma((7,)),
            dma((4,)),
            dma((4,)),
            dma((4,)),
            dma((4,)),
            dma((2,)),
            dma((2,)),
            dma((3,)),
        ],
        compiler_params=pltpu.CompilerParams(
            collective_id=0, has_side_effects=True, vmem_limit_bytes=56 << 20
        ),
        name="spectral_block",
    )(
        spectra.reshape(8, C, MODES),
        cotangent.reshape(8, C, MODES),
        weights,
        jnp.asarray(fb),
        jnp.asarray(fbt),
        jnp.asarray(ei),
        jnp.asarray(eo),
    )
    shape = (1, 2, 4, C, MODES)
    return out.reshape(shape), gin.reshape(shape), wg


def solution(mesh):
    field = P("ba", None, "gx", None, None)
    return jax.shard_map(
        on_device,
        mesh=mesh,
        in_specs=(field, field, P("gx", None)),
        out_specs=(field, field, P("gx", None)),
        check_vma=False,
    )
```

```python
import functools
import math

import jax
import jax.numpy as jnp
import numpy as np
from jax import lax
from jax.experimental import pallas as pl
from jax.experimental.pallas import tpu as pltpu
from jax.sharding import PartitionSpec as P

C = 20
X = 256
KX = 24
SHARD = 54
MODES = 3456
TILES = MODES // 128
PLANE = 32
COLS = 1152
NT = COLS // 128
GROUP = 8
GN = GROUP * C * C
MESH = pl.DeviceIdType.MESH


def table():
    mode = np.arange(KX)
    wave = np.where(mode < KX // 2, mode, mode - KX)
    phases = wave[:, None] * np.arange(X)[None, :] % X
    angles = phases.astype(np.float32) * np.float32(2.0 * math.pi / X)
    factor = np.float32(1.0 / math.sqrt(X))
    c = np.cos(angles) * factor
    s = np.sin(angles) * factor
    full = np.concatenate([np.concatenate([c, s], 1), np.concatenate([-s, c], 1)], 0)
    return full.astype(jnp.bfloat16).astype(np.float32)


@functools.cache
def constants():
    f = table().reshape(2, 3, GROUP, 2, 2, PLANE, 4)
    f = f.transpose(4, 1, 0, 2, 5, 3, 6)
    fb = np.zeros((2, 2, 48, PLANE, 2, 8), np.float32)
    for z in range(2):
        rows = f[z].reshape(48, PLANE, 8)
        fb[z, 0, :, :, z] = rows
        fb[z, 1, :, :, 1 - z] = rows
    fb = fb.reshape(2, 96, 512)
    bf = lambda a: a.astype(jnp.bfloat16)
    return bf(fb), bf(fb.transpose(0, 2, 1))


def spot(c):
    return 54 * c // 128, 54 * c % 128


def kernel(
    x_hbm, ct_hbm, w_hbm, fb_hbm, fbt_hbm,
    out_hbm, gin_hbm, wg_hbm,
    xb, xs, w, fb, fbt, sbuf, rbuf, zs, zr, coef, vt, vp, vq, wt, mt, ga, gb, wgt, wg, ob,
    load_sem, ssem, rsem, zssem, zrsem, bssem, brsem, out_sem,
):
    me = lax.axis_index("gx")
    ba = lax.axis_index("ba")
    z = me // PLANE
    q = me % PLANE
    qx, qy, qc = q // 8, q // 2 % 4, q % 2

    def peer(j):
        i = j // 2
        return (qx + i) % 4 * 8 + (qy + i // 4 + i) % 4 * 2 + (qc + j) % 2

    def load(i, src, dst):
        copy = pltpu.make_async_copy(src, dst, load_sem.at[i])
        copy.start()
        return copy

    loads = [
        load(0, x_hbm, xb.at[0]),
        load(1, ct_hbm, xb.at[1]),
        load(2, fb_hbm, fb),
        load(3, w_hbm, w),
        load(4, fbt_hbm, fbt),
    ]

    bar = pltpu.get_barrier_semaphore()

    def greet(j, carry):
        pl.semaphore_signal(bar, inc=1, device_id=(z * PLANE + peer(j), ba), device_id_type=MESH)
        return carry

    lax.fori_loop(1, PLANE, greet, 0)
    zpeer = ((1 - z) * PLANE + q, ba)
    pl.semaphore_signal(bar, inc=1, device_id=zpeer, device_id_type=MESH)
    for d in range(1, 4):
        pl.semaphore_signal(bar, inc=1, device_id=(me, (ba + d) % 4), device_id_type=MESH)

    lane = lax.broadcasted_iota(jnp.int32, (8, 128), 1)
    lane16 = lax.broadcasted_iota(jnp.int16, (16, 128), 1)

    def rows8(which, c, cols):
        return jnp.concatenate(
            [xb[which, p, c, :, cols].astype(jnp.float32) for p in range(2)], axis=0
        )

    def arrange(which):
        def tile(t, carry):
            def cols(u):
                return pl.ds(pl.multiple_of(jnp.minimum(u, TILES - 1) * 128, 128), 128)

            for c in range(C):
                low = rows8(which, c, cols(t))
                high = jnp.where(
                    lane >= 64, rows8(which, c, cols(t + 13)), rows8(which, c, cols(t + 14))
                )
                both = jnp.concatenate([low, pltpu.roll(high, 64, 1)], axis=0)
                xs[t, 16 * c : 16 * c + 16, :] = both.astype(jnp.bfloat16)
            return carry

        lax.fori_loop(0, 14, tile, 0)

    def pack(dest, store):
        lane0 = 54 * dest
        t0 = lane0 // 128
        amt = lane0 % 128
        t1 = jnp.minimum(t0 + 1, 13)
        mask = lane16 >= amt.astype(jnp.int16)
        merged = jnp.concatenate(
            [
                jnp.where(mask, xs[t0, 16 * c : 16 * c + 16, :], xs[t1, 16 * c : 16 * c + 16, :])
                for c in range(C)
            ],
            axis=0,
        )
        merged = pltpu.roll(merged, (128 - amt) % 128, 1)
        tiles = [None] * NT
        for c in range(C):
            T, pos = spot(c)
            v = merged[16 * c : 16 * c + 16]
            if pos:
                v = pltpu.roll(v, pos, 1)
            tiles[T] = v if pos == 0 else jnp.where(lane16 >= pos, v, tiles[T])
            if pos + 54 > 128:
                tiles[T + 1] = v
        for T in range(NT):
            store(T, tiles[T])

    def send(phase, dest):
        pltpu.make_async_remote_copy(
            src_ref=sbuf.at[phase, dest],
            dst_ref=rbuf.at[phase, q],
            send_sem=ssem.at[phase],
            recv_sem=rsem.at[phase],
            device_id=(z * PLANE + dest, ba),
            device_id_type=MESH,
        ).start()

    def received(phase):
        part = rbuf.at[phase, pl.ds(0, PLANE - 1)]
        pltpu.make_async_copy(part, part, rsem.at[phase]).wait()

    def scatter(phase):
        def own(T, value):
            rbuf[phase, q, :, T * 128 : T * 128 + 128] = value

        pack(q, own)

        def step(j, carry):
            dest = peer(j)

            def put(T, value):
                sbuf[phase, dest, :, T * 128 : T * 128 + 128] = value

            pack(dest, put)
            send(phase, dest)
            return carry

        lax.fori_loop(1, PLANE, step, 0)

    def swap(slot, g):
        part = (slot, pl.ds(16 * g, 16))
        copy = pltpu.make_async_remote_copy(
            src_ref=zs.at[part], dst_ref=zr.at[part], send_sem=zssem.at[slot, g],
            recv_sem=zrsem.at[slot, g], device_id=zpeer, device_id_type=MESH,
        )
        copy.start()
        return copy

    def transform(phase):
        rows = rbuf[phase].reshape(512, COLS)
        part = jnp.dot(fb[z, 48:96], rows, preferred_element_type=jnp.float32)
        zs[phase] = part.astype(jnp.bfloat16)
        copies = [swap(phase, g) for g in range(3)]
        swaps.extend(copies)
        mine = jnp.dot(fb[z, 0:48], rows, preferred_element_type=jnp.float32)
        return copies, mine

    def turn(phase, copies, mine):
        for g in range(3):
            copies[g].wait_recv()
            got = zr[phase, 16 * g : 16 * g + 16].astype(jnp.float32)
            full = (mine[16 * g : 16 * g + 16] + got).astype(jnp.bfloat16).astype(jnp.float32)
            tiles = [full[:, T * 128 : T * 128 + 128] for T in range(NT)]
            for c in range(C):
                T, pos = spot(c)
                halves = []
                for p in range(2):
                    v = tiles[T][8 * p : 8 * p + 8]
                    if pos + 54 > 128:
                        v = jnp.where(lane >= pos, v, tiles[T + 1][8 * p : 8 * p + 8])
                    shift = (128 + 64 * p - pos) % 128
                    halves.append(pltpu.roll(v, shift, 1) if shift else v)
                v = jnp.where(lane < 64, halves[0], halves[1])
                turned = pltpu.roll(v, 64, 1)
                rows = pl.ds(8 * g * C + c, 8, stride=C)
                vt[rows, :] = v
                if phase == 0:
                    vp[rows, :] = jnp.where(lane < 64, v, -v)
                    vq[rows, :] = turned
                else:
                    vp[rows, :] = v
                    vq[rows, :] = jnp.where(lane < 64, turned, -turned)
        coef[phase, ba] = vt[...].astype(jnp.bfloat16)

    def gather(phase):
        for d in range(1, 4):
            pltpu.make_async_remote_copy(
                src_ref=coef.at[phase, ba], dst_ref=coef.at[phase, ba],
                send_sem=bssem.at[phase], recv_sem=brsem.at[phase],
                device_id=(me, (ba + d) % 4), device_id_type=MESH,
            ).start()

    def gathered(phase):
        part = coef.at[phase, pl.ds(0, 3)]
        pltpu.make_async_copy(part, part, brsem.at[phase]).wait()
        pltpu.make_async_copy(part, part, bssem.at[phase]).wait()

    def turn_weights():
        r = lax.broadcasted_iota(jnp.int32, (128, 128), 0)
        eye = (r == lax.broadcasted_iota(jnp.int32, (128, 128), 1)).astype(jnp.bfloat16)
        zero = jnp.zeros((10, 128), jnp.float32)

        def one(j, carry):
            n0 = pl.multiple_of(j * 128, 128)
            wr = w[:, pl.ds(n0, 128)].astype(jnp.float32)
            wi = w[:, pl.ds(pl.multiple_of(n0 + 3 * GN, 128), 128)].astype(jnp.float32)
            both = jnp.concatenate([wr, zero, wi, zero], axis=0).astype(jnp.bfloat16)
            wt[pl.ds(n0, 128), :] = lax.dot_general(
                eye, both, (((1,), (1,)), ((), ())), preferred_element_type=jnp.float32
            )
            return carry

        lax.fori_loop(0, 3 * GN // 128, one, 0, unroll=5)

    def mix(phase, slot):
        low = lax.broadcasted_iota(jnp.int32, (C, 128), 1) < 64
        for g in range(3):

            def one(kk, carry):
                k = 8 * g + kk
                base = pl.multiple_of(k * (C * C), 8)
                first = second = jnp.zeros((C, 128), jnp.float32)
                for j in range(C):
                    if phase == 0:
                        rows = wt[pl.ds(base + C * j, C), :]
                    else:
                        rows = wt[pl.ds(base + j, C, stride=C), :]
                    first = first + vp[pl.ds(k * C + j, 1), :] * rows
                    second = second + vq[pl.ds(k * C + j, 1), :] * rows
                first = first + pltpu.roll(first, 64, 1)
                second = second + pltpu.roll(second, 64, 1)
                mt[pl.ds(pl.multiple_of(24 * k, 8), C), :] = jnp.where(low, first, second)
                return carry

            lax.fori_loop(0, 8, one, 0)
            halves = [[None] * NT, [None] * NT]
            for c in range(C):
                T, pos = spot(c)
                v = mt[pl.ds(8 * g * 24 + c, 8, stride=24), :]
                for p in range(2):
                    shift = (pos + 64 * p) % 128
                    u = pltpu.roll(v, shift, 1) if shift else v
                    tiles = halves[p]
                    tiles[T] = u if pos == 0 else jnp.where(lane >= pos, u, tiles[T])
                    if pos + 54 > 128:
                        tiles[T + 1] = u
            for T in range(NT):
                both = jnp.concatenate([halves[0][T], halves[1][T]], axis=0)
                zs[slot, 16 * g : 16 * g + 16, T * 128 : T * 128 + 128] = both.astype(jnp.bfloat16)
            swaps.append(swap(slot, g))
        return swaps[-3:]

    def invert(phase, slot, copies):
        for copy in copies:
            copy.wait_recv()
        modes = jnp.concatenate([zs[slot], zr[slot]], axis=0)
        step = 128
        for b in range(512 // step):
            rows = jnp.dot(
                fbt[z, b * step : b * step + step, :], modes, preferred_element_type=jnp.float32
            )
            first = b * step // 16
            sbuf[phase, first : first + step // 16] = rows.astype(jnp.bfloat16).reshape(
                step // 16, 16, COLS
            )
        rbuf[phase, q] = sbuf[phase, q]

        def one(j, carry):
            send(phase, peer(j))
            return carry

        lax.fori_loop(1, PLANE, one, 0)

    def unpack(phase, slot, dst):
        def one(source, carry):
            lane0 = 54 * source
            t0 = lane0 // 128
            amt = lane0 % 128
            mask = lane16 >= amt.astype(jnp.int16)
            tiles = [rbuf[phase, source, :, T * 128 : T * 128 + 128] for T in range(NT)]
            pieces = []
            for c in range(C):
                T, pos = spot(c)
                v = tiles[T]
                if pos + 54 > 128:
                    v = jnp.where(lane16 >= pos, v, tiles[T + 1])
                pieces.append(pltpu.roll(v, 128 - pos, 1) if pos else v)
            merged = pltpu.roll(jnp.concatenate(pieces, axis=0), amt, 1)
            for c in range(C):
                rows = slice(16 * c, 16 * c + 16)
                v = merged[rows]
                xs[t0, rows, :] = jnp.where(mask, v, xs[t0, rows, :])
                xs[t0 + 1, rows, :] = v
            return carry

        lax.fori_loop(0, PLANE, one, 0)

        def put(t, c, value):
            cols = pl.ds(pl.multiple_of(t * 128, 128), 128)
            for p in range(2):
                ob[slot, p, c, :, cols] = value[4 * p : 4 * p + 4].astype(jnp.bfloat16)

        def tile(t, carry):
            for c in range(C):
                rows = slice(16 * c, 16 * c + 16)
                here = xs[t, rows, :].astype(jnp.float32)
                after = xs[t + 1, rows, :].astype(jnp.float32)
                put(t, c, here[0:8])
                high = jnp.where(lane >= 64, here[8:16], after[8:16])
                put(t + 14, c, pltpu.roll(high, 64, 1))
            return carry

        lax.fori_loop(0, 13, tile, 0)
        for c in range(C):
            rows = slice(16 * c, 16 * c + 16)
            high = pltpu.roll(xs[0, rows, :].astype(jnp.float32)[8:16], 64, 1)
            low = xs[13, rows, :].astype(jnp.float32)[0:8]
            put(13, c, jnp.where(lane < 64, low, high))
        copy = pltpu.make_async_copy(ob.at[slot], dst, out_sem.at[slot])
        copy.start()
        return copy

    def outer():
        low = lax.broadcasted_iota(jnp.int32, (24 * C, 128), 1) < 64
        for s in range(4):
            a = coef[0, s].astype(jnp.float32)
            turned = pltpu.roll(a, 64, 1)
            ga[s, 0] = jnp.where(low, a, turned)
            ga[s, 1] = jnp.where(low, turned, a)
            b = coef[1, s].astype(jnp.float32)
            turned = pltpu.roll(b, 64, 1)
            gb[s, 0] = b
            gb[s, 1] = jnp.where(low, turned, -turned)

        def one(k, carry):
            base = pl.multiple_of(k * (C * C), 8)
            right = [[gb[s, u, pl.ds(k * C, C), :] for u in range(2)] for s in range(4)]
            for i in range(C):
                total = None
                for s in range(4):
                    for u in range(2):
                        term = ga[s, u, pl.ds(k * C + i, 1), :] * right[s][u]
                        total = term if total is None else total + term
                wgt[pl.ds(base + C * i, C), :] = total
            return carry

        lax.fori_loop(0, KX, one, 0)

        def flip(j, carry):
            n0 = pl.multiple_of(j * 128, 128)
            both = wgt[pl.ds(n0, 128), :].T
            wg[:, pl.ds(n0, 128)] = both[0:54]
            wg[:, pl.ds(pl.multiple_of(n0 + 3 * GN, 128), 128)] = both[64:118]
            return carry

        lax.fori_loop(0, 3 * GN // 128, flip, 0, unroll=5)
        copy = pltpu.make_async_copy(wg, wg_hbm, out_sem.at[2])
        copy.start()
        return copy

    swaps = []
    loads[0].wait()
    arrange(0)
    pl.semaphore_wait(bar, PLANE - 1 + 1 + 3)
    scatter(0)
    loads[1].wait()
    arrange(1)
    scatter(1)
    for copy in loads[2:]:
        copy.wait()
    turn_weights()
    received(0)
    turn(0, *transform(0))
    back = mix(0, 2)
    received(1)
    front = transform(1)
    invert(2, 2, back)
    gather(0)
    turn(1, *front)
    back = mix(1, 3)
    gather(1)
    invert(3, 3, back)
    received(2)
    done = [unpack(2, 0, out_hbm)]
    gathered(0)
    gathered(1)
    done.append(outer())
    received(3)
    done.append(unpack(3, 1, gin_hbm))
    for copy in swaps:
        copy.wait_send()
    for phase in range(4):
        part = sbuf.at[phase, pl.ds(0, PLANE - 1)]
        pltpu.make_async_copy(part, part, ssem.at[phase]).wait()
    for copy in done:
        copy.wait()


def on_device(spectra, cotangent, weights):
    fb, fbt = constants()
    bf, f32 = jnp.bfloat16, jnp.float32
    vm = pltpu.VMEM
    dma = pltpu.SemaphoreType.DMA
    out, gin, wg = pl.pallas_call(
        kernel,
        out_shape=[
            jax.ShapeDtypeStruct((2, C, 4, MODES), bf),
            jax.ShapeDtypeStruct((2, C, 4, MODES), bf),
            jax.ShapeDtypeStruct((SHARD, 6 * GN), f32),
        ],
        in_specs=[pl.BlockSpec(memory_space=pl.ANY)] * 5,
        out_specs=[pl.BlockSpec(memory_space=pl.ANY)] * 3,
        scratch_shapes=[
            vm((2, 2, C, 4, MODES), bf),
            vm((15, 16 * C, 128), bf),
            vm((SHARD, 6 * GN), bf),
            vm((2, 96, 512), bf),
            vm((2, 512, 96), bf),
            vm((4, PLANE, 16, COLS), bf),
            vm((4, PLANE, 16, COLS), bf),
            vm((4, 48, COLS), bf),
            vm((4, 48, COLS), bf),
            vm((2, 4, KX * C, 128), bf),
            vm((KX * C, 128), f32),
            vm((KX * C, 128), f32),
            vm((KX * C, 128), f32),
            vm((3 * GN, 128), f32),
            vm((KX * 24, 128), f32),
            vm((4, 2, KX * C, 128), f32),
            vm((4, 2, KX * C, 128), f32),
            vm((3 * GN, 128), f32),
            vm((SHARD, 6 * GN), f32),
            vm((2, 2, C, 4, MODES), bf),
            dma((5,)),
            dma((4,)),
            dma((4,)),
            dma((4, 3)),
            dma((4, 3)),
            dma((2,)),
            dma((2,)),
            dma((3,)),
        ],
        compiler_params=pltpu.CompilerParams(
            collective_id=0, has_side_effects=True, vmem_limit_bytes=56 << 20
        ),
        name="spectral_block",
    )(
        spectra[0].swapaxes(1, 2),
        cotangent[0].swapaxes(1, 2),
        weights,
        jnp.asarray(fb),
        jnp.asarray(fbt),
    )
    return out.swapaxes(1, 2)[None], gin.swapaxes(1, 2)[None], wg


def solution(mesh):
    field = P("ba", None, "gx", None, None)
    return jax.shard_map(
        on_device,
        mesh=mesh,
        in_specs=(field, field, P("gx", None)),
        out_specs=(field, field, P("gx", None)),
        check_vma=False,
    )
```

```python
import functools
import math

import jax
import jax.numpy as jnp
import numpy as np
from jax import lax
from jax.experimental import pallas as pl
from jax.experimental.pallas import tpu as pltpu
from jax.sharding import PartitionSpec as P

C = 20
X = 256
KX = 24
SHARD = 54
MODES = 3456
TILES = MODES // 128
PLANE = 32
COLS = 1152
NT = COLS // 128
GROUP = 8
GN = GROUP * C * C
MESH = pl.DeviceIdType.MESH


def table():
    mode = np.arange(KX)
    wave = np.where(mode < KX // 2, mode, mode - KX)
    phases = wave[:, None] * np.arange(X)[None, :] % X
    angles = phases.astype(np.float32) * np.float32(2.0 * math.pi / X)
    factor = np.float32(1.0 / math.sqrt(X))
    c = np.cos(angles) * factor
    s = np.sin(angles) * factor
    full = np.concatenate([np.concatenate([c, s], 1), np.concatenate([-s, c], 1)], 0)
    return full.astype(jnp.bfloat16).astype(np.float32)


@functools.cache
def constants():
    f = table().reshape(2, 3, GROUP, 2, 2, PLANE, 4)
    f = f.transpose(4, 1, 0, 2, 5, 3, 6)
    fb = np.zeros((2, 2, 48, PLANE, 2, 8), np.float32)
    for z in range(2):
        rows = f[z].reshape(48, PLANE, 8)
        fb[z, 0, :, :, z] = rows
        fb[z, 1, :, :, 1 - z] = rows
    fb = fb.reshape(2, 96, 512)
    bf = lambda a: a.astype(jnp.bfloat16)
    return bf(fb), bf(fb.transpose(0, 2, 1))


def spot(c):
    return 54 * c // 128, 54 * c % 128


def kernel(
    x_hbm, ct_hbm, w_hbm, fb_hbm, fbt_hbm,
    out_hbm, gin_hbm, wg_hbm,
    xb, xs, w, fb, fbt, sbuf, rbuf, zs, zr, coef, vt, vp, vq, wt, mt, ga, gb, wgt, wg, ob,
    load_sem, ssem, rsem, zssem, zrsem, bssem, brsem, out_sem,
):
    me = lax.axis_index("gx")
    ba = lax.axis_index("ba")
    z = me // PLANE
    q = me % PLANE
    qx, qy, qc = q // 8, q // 2 % 4, q % 2

    def peer(j):
        i = j // 2
        return (qx + i) % 4 * 8 + (qy + i // 4 + i) % 4 * 2 + (qc + j) % 2

    def load(i, src, dst):
        copy = pltpu.make_async_copy(src, dst, load_sem.at[i])
        copy.start()
        return copy

    loads = [
        load(0, x_hbm, xb.at[0]),
        load(1, ct_hbm, xb.at[1]),
        load(2, fb_hbm, fb),
        load(3, w_hbm, w),
        load(4, fbt_hbm, fbt),
    ]

    bar = pltpu.get_barrier_semaphore()

    def greet(j, carry):
        pl.semaphore_signal(bar, inc=1, device_id=(z * PLANE + peer(j), ba), device_id_type=MESH)
        return carry

    lax.fori_loop(1, PLANE, greet, 0)
    zpeer = ((1 - z) * PLANE + q, ba)
    pl.semaphore_signal(bar, inc=1, device_id=zpeer, device_id_type=MESH)
    for d in range(1, 4):
        pl.semaphore_signal(bar, inc=1, device_id=(me, (ba + d) % 4), device_id_type=MESH)

    lane = lax.broadcasted_iota(jnp.int32, (8, 128), 1)
    lane16 = lax.broadcasted_iota(jnp.int16, (16, 128), 1)

    def rows8(which, c, cols):
        return jnp.concatenate(
            [xb[which, p, c, :, cols].astype(jnp.float32) for p in range(2)], axis=0
        )

    def arrange(which):
        def tile(t, carry):
            def cols(u):
                return pl.ds(pl.multiple_of(jnp.minimum(u, TILES - 1) * 128, 128), 128)

            for c in range(C):
                low = rows8(which, c, cols(t))
                high = jnp.where(
                    lane >= 64, rows8(which, c, cols(t + 13)), rows8(which, c, cols(t + 14))
                )
                both = jnp.concatenate([low, pltpu.roll(high, 64, 1)], axis=0)
                xs[t, 16 * c : 16 * c + 16, :] = both.astype(jnp.bfloat16)
            return carry

        lax.fori_loop(0, 14, tile, 0)

    def pack(dest, store):
        lane0 = 54 * dest
        t0 = lane0 // 128
        amt = lane0 % 128
        t1 = jnp.minimum(t0 + 1, 13)
        mask = lane16 >= amt.astype(jnp.int16)
        merged = jnp.concatenate(
            [
                jnp.where(mask, xs[t0, 16 * c : 16 * c + 16, :], xs[t1, 16 * c : 16 * c + 16, :])
                for c in range(C)
            ],
            axis=0,
        )
        merged = pltpu.roll(merged, (128 - amt) % 128, 1)
        tiles = [None] * NT
        for c in range(C):
            T, pos = spot(c)
            v = merged[16 * c : 16 * c + 16]
            if pos:
                v = pltpu.roll(v, pos, 1)
            tiles[T] = v if pos == 0 else jnp.where(lane16 >= pos, v, tiles[T])
            if pos + 54 > 128:
                tiles[T + 1] = v
        for T in range(NT):
            store(T, tiles[T])

    def send(phase, dest):
        pltpu.make_async_remote_copy(
            src_ref=sbuf.at[phase, dest],
            dst_ref=rbuf.at[phase, q],
            send_sem=ssem.at[phase],
            recv_sem=rsem.at[phase],
            device_id=(z * PLANE + dest, ba),
            device_id_type=MESH,
        ).start()

    def received(phase):
        part = rbuf.at[phase, pl.ds(0, PLANE - 1)]
        pltpu.make_async_copy(part, part, rsem.at[phase]).wait()

    def scatter(phase):
        def own(T, value):
            rbuf[phase, q, :, T * 128 : T * 128 + 128] = value

        pack(q, own)

        def step(j, carry):
            dest = peer(j)

            def put(T, value):
                sbuf[phase, dest, :, T * 128 : T * 128 + 128] = value

            pack(dest, put)
            send(phase, dest)
            return carry

        lax.fori_loop(1, PLANE, step, 0)

    def swap(slot, g):
        part = (slot, pl.ds(16 * g, 16))
        copy = pltpu.make_async_remote_copy(
            src_ref=zs.at[part], dst_ref=zr.at[part], send_sem=zssem.at[slot, g],
            recv_sem=zrsem.at[slot, g], device_id=zpeer, device_id_type=MESH,
        )
        copy.start()
        return copy

    def transform(phase):
        rows = rbuf[phase].reshape(512, COLS)
        part = jnp.dot(fb[z, 48:96], rows, preferred_element_type=jnp.float32)
        zs[phase] = part.astype(jnp.bfloat16)
        copies = [swap(phase, g) for g in range(3)]
        swaps.extend(copies)
        mine = jnp.dot(fb[z, 0:48], rows, preferred_element_type=jnp.float32)
        return copies, mine

    def turn(phase, copies, mine):
        for g in range(3):
            copies[g].wait_recv()
            got = zr[phase, 16 * g : 16 * g + 16].astype(jnp.float32)
            full = (mine[16 * g : 16 * g + 16] + got).astype(jnp.bfloat16).astype(jnp.float32)
            tiles = [full[:, T * 128 : T * 128 + 128] for T in range(NT)]
            for c in range(C):
                T, pos = spot(c)
                halves = []
                for p in range(2):
                    v = tiles[T][8 * p : 8 * p + 8]
                    if pos + 54 > 128:
                        v = jnp.where(lane >= pos, v, tiles[T + 1][8 * p : 8 * p + 8])
                    shift = (128 + 64 * p - pos) % 128
                    halves.append(pltpu.roll(v, shift, 1) if shift else v)
                v = jnp.where(lane < 64, halves[0], halves[1])
                turned = pltpu.roll(v, 64, 1)
                rows = pl.ds(8 * g * C + c, 8, stride=C)
                vt[rows, :] = v
                if phase == 0:
                    vp[rows, :] = jnp.where(lane < 64, v, -v)
                    vq[rows, :] = turned
                else:
                    vp[rows, :] = v
                    vq[rows, :] = jnp.where(lane < 64, turned, -turned)
        coef[phase, ba] = vt[...].astype(jnp.bfloat16)

    def gather(phase):
        for d in range(1, 4):
            pltpu.make_async_remote_copy(
                src_ref=coef.at[phase, ba], dst_ref=coef.at[phase, ba],
                send_sem=bssem.at[phase], recv_sem=brsem.at[phase],
                device_id=(me, (ba + d) % 4), device_id_type=MESH,
            ).start()

    def gathered(phase):
        part = coef.at[phase, pl.ds(0, 3)]
        pltpu.make_async_copy(part, part, brsem.at[phase]).wait()
        pltpu.make_async_copy(part, part, bssem.at[phase]).wait()

    def turn_weights():
        r = lax.broadcasted_iota(jnp.int32, (128, 128), 0)
        eye = (r == lax.broadcasted_iota(jnp.int32, (128, 128), 1)).astype(jnp.bfloat16)
        zero = jnp.zeros((10, 128), jnp.float32)

        def one(j, carry):
            n0 = pl.multiple_of(j * 128, 128)
            wr = w[:, pl.ds(n0, 128)].astype(jnp.float32)
            wi = w[:, pl.ds(pl.multiple_of(n0 + 3 * GN, 128), 128)].astype(jnp.float32)
            both = jnp.concatenate([wr, zero, wi, zero], axis=0).astype(jnp.bfloat16)
            wt[pl.ds(n0, 128), :] = lax.dot_general(
                eye, both, (((1,), (1,)), ((), ())), preferred_element_type=jnp.float32
            )
            return carry

        lax.fori_loop(0, 3 * GN // 128, one, 0, unroll=5)

    def mix(phase, slot):
        low = lax.broadcasted_iota(jnp.int32, (C, 128), 1) < 64
        for g in range(3):

            def one(kk, carry):
                k = 8 * g + kk
                base = pl.multiple_of(k * (C * C), 8)
                first = second = jnp.zeros((C, 128), jnp.float32)
                for j in range(C):
                    if phase == 0:
                        rows = wt[pl.ds(base + C * j, C), :]
                    else:
                        rows = wt[pl.ds(base + j, C, stride=C), :]
                    first = first + vp[pl.ds(k * C + j, 1), :] * rows
                    second = second + vq[pl.ds(k * C + j, 1), :] * rows
                first = first + pltpu.roll(first, 64, 1)
                second = second + pltpu.roll(second, 64, 1)
                mt[pl.ds(pl.multiple_of(24 * k, 8), C), :] = jnp.where(low, first, second)
                return carry

            lax.fori_loop(0, 8, one, 0)
            halves = [[None] * NT, [None] * NT]
            for c in range(C):
                T, pos = spot(c)
                v = mt[pl.ds(8 * g * 24 + c, 8, stride=24), :]
                for p in range(2):
                    shift = (pos + 64 * p) % 128
                    u = pltpu.roll(v, shift, 1) if shift else v
                    tiles = halves[p]
                    tiles[T] = u if pos == 0 else jnp.where(lane >= pos, u, tiles[T])
                    if pos + 54 > 128:
                        tiles[T + 1] = u
            for T in range(NT):
                both = jnp.concatenate([halves[0][T], halves[1][T]], axis=0)
                zs[slot, 16 * g : 16 * g + 16, T * 128 : T * 128 + 128] = both.astype(jnp.bfloat16)
            swaps.append(swap(slot, g))
        return swaps[-3:]

    def invert(phase, slot, copies):
        for copy in copies:
            copy.wait_recv()
        modes = jnp.concatenate([zs[slot], zr[slot]], axis=0)
        step = 128
        for b in range(512 // step):
            rows = jnp.dot(
                fbt[z, b * step : b * step + step, :], modes, preferred_element_type=jnp.float32
            )
            first = b * step // 16
            sbuf[phase, first : first + step // 16] = rows.astype(jnp.bfloat16).reshape(
                step // 16, 16, COLS
            )
        rbuf[phase, q] = sbuf[phase, q]

        def one(j, carry):
            send(phase, peer(j))
            return carry

        lax.fori_loop(1, PLANE, one, 0)

    def unpack(phase, slot, dst):
        def one(source, carry):
            lane0 = 54 * source
            t0 = lane0 // 128
            amt = lane0 % 128
            mask = lane16 >= amt.astype(jnp.int16)
            tiles = [rbuf[phase, source, :, T * 128 : T * 128 + 128] for T in range(NT)]
            pieces = []
            for c in range(C):
                T, pos = spot(c)
                v = tiles[T]
                if pos + 54 > 128:
                    v = jnp.where(lane16 >= pos, v, tiles[T + 1])
                pieces.append(pltpu.roll(v, 128 - pos, 1) if pos else v)
            merged = pltpu.roll(jnp.concatenate(pieces, axis=0), amt, 1)
            for c in range(C):
                rows = slice(16 * c, 16 * c + 16)
                v = merged[rows]
                xs[t0, rows, :] = jnp.where(mask, v, xs[t0, rows, :])
                xs[t0 + 1, rows, :] = v
            return carry

        lax.fori_loop(0, PLANE, one, 0, unroll=4)

        def put(t, c, value):
            cols = pl.ds(pl.multiple_of(t * 128, 128), 128)
            for p in range(2):
                ob[slot, p, c, :, cols] = value[4 * p : 4 * p + 4].astype(jnp.bfloat16)

        def tile(t, carry):
            for c in range(C):
                rows = slice(16 * c, 16 * c + 16)
                here = xs[t, rows, :].astype(jnp.float32)
                after = xs[t + 1, rows, :].astype(jnp.float32)
                put(t, c, here[0:8])
                high = jnp.where(lane >= 64, here[8:16], after[8:16])
                put(t + 14, c, pltpu.roll(high, 64, 1))
            return carry

        lax.fori_loop(0, 13, tile, 0)
        for c in range(C):
            rows = slice(16 * c, 16 * c + 16)
            high = pltpu.roll(xs[0, rows, :].astype(jnp.float32)[8:16], 64, 1)
            low = xs[13, rows, :].astype(jnp.float32)[0:8]
            put(13, c, jnp.where(lane < 64, low, high))
        copy = pltpu.make_async_copy(ob.at[slot], dst, out_sem.at[slot])
        copy.start()
        return copy

    def outer():
        low = lax.broadcasted_iota(jnp.int32, (24 * C, 128), 1) < 64
        for s in range(4):
            a = coef[0, s].astype(jnp.float32)
            turned = pltpu.roll(a, 64, 1)
            ga[s, 0] = jnp.where(low, a, turned)
            ga[s, 1] = jnp.where(low, turned, a)
            b = coef[1, s].astype(jnp.float32)
            turned = pltpu.roll(b, 64, 1)
            gb[s, 0] = b
            gb[s, 1] = jnp.where(low, turned, -turned)

        def one(k, carry):
            base = pl.multiple_of(k * (C * C), 8)
            right = [[gb[s, u, pl.ds(k * C, C), :] for u in range(2)] for s in range(4)]
            for i in range(C):
                total = None
                for s in range(4):
                    for u in range(2):
                        term = ga[s, u, pl.ds(k * C + i, 1), :] * right[s][u]
                        total = term if total is None else total + term
                wgt[pl.ds(base + C * i, C), :] = total
            return carry

        lax.fori_loop(0, KX, one, 0)

        def flip(j, carry):
            n0 = pl.multiple_of(j * 128, 128)
            both = wgt[pl.ds(n0, 128), :].T
            wg[:, pl.ds(n0, 128)] = both[0:54]
            wg[:, pl.ds(pl.multiple_of(n0 + 3 * GN, 128), 128)] = both[64:118]
            return carry

        lax.fori_loop(0, 3 * GN // 128, flip, 0, unroll=5)
        copy = pltpu.make_async_copy(wg, wg_hbm, out_sem.at[2])
        copy.start()
        return copy

    swaps = []
    loads[0].wait()
    arrange(0)
    pl.semaphore_wait(bar, PLANE - 1 + 1 + 3)
    scatter(0)
    loads[1].wait()
    arrange(1)
    scatter(1)
    for copy in loads[2:]:
        copy.wait()
    turn_weights()
    received(0)
    turn(0, *transform(0))
    back = mix(0, 2)
    received(1)
    front = transform(1)
    invert(2, 2, back)
    gather(0)
    turn(1, *front)
    back = mix(1, 3)
    gather(1)
    invert(3, 3, back)
    received(2)
    done = [unpack(2, 0, out_hbm)]
    gathered(0)
    gathered(1)
    done.append(outer())
    received(3)
    done.append(unpack(3, 1, gin_hbm))
    for copy in swaps:
        copy.wait_send()
    for phase in range(4):
        part = sbuf.at[phase, pl.ds(0, PLANE - 1)]
        pltpu.make_async_copy(part, part, ssem.at[phase]).wait()
    for copy in done:
        copy.wait()


def hand_over(a, b, c, to_a, to_b, to_c, va, vb, vc, sem, sem_out):
    parts = []
    for first, rows in ((0, 16), (16, 16), (32, 16), (48, 6)):
        parts.append((c, vc, to_c, (pl.ds(first, rows),)))
    for src, mid, dst in ((a, va, to_a), (b, vb, to_b)):
        for p in range(2):
            parts.append((src, mid, dst, (p,)))
    loads = []
    for n, (src, mid, dst, part) in enumerate(parts):
        loads.append(pltpu.make_async_copy(src.at[part], mid.at[part], sem.at[n]))
        loads[-1].start()
    stores = []
    for n, (src, mid, dst, part) in enumerate(parts):
        loads[n].wait()
        stores.append(pltpu.make_async_copy(mid.at[part], dst.at[part], sem_out.at[n]))
        stores[-1].start()
    for copy in stores:
        copy.wait()


def on_device(spectra, cotangent, weights):
    fb, fbt = constants()
    bf, f32 = jnp.bfloat16, jnp.float32
    vm = pltpu.VMEM
    dma = pltpu.SemaphoreType.DMA
    out, gin, wg = pl.pallas_call(
        kernel,
        out_shape=[
            jax.ShapeDtypeStruct((2, C, 4, MODES), bf),
            jax.ShapeDtypeStruct((2, C, 4, MODES), bf),
            jax.ShapeDtypeStruct((SHARD, 6 * GN), f32),
        ],
        in_specs=[pl.BlockSpec(memory_space=pl.ANY)] * 5,
        out_specs=[pl.BlockSpec(memory_space=pl.ANY)] * 3,
        scratch_shapes=[
            vm((2, 2, C, 4, MODES), bf),
            vm((15, 16 * C, 128), bf),
            vm((SHARD, 6 * GN), bf),
            vm((2, 96, 512), bf),
            vm((2, 512, 96), bf),
            vm((4, PLANE, 16, COLS), bf),
            vm((4, PLANE, 16, COLS), bf),
            vm((4, 48, COLS), bf),
            vm((4, 48, COLS), bf),
            vm((2, 4, KX * C, 128), bf),
            vm((KX * C, 128), f32),
            vm((KX * C, 128), f32),
            vm((KX * C, 128), f32),
            vm((3 * GN, 128), f32),
            vm((KX * 24, 128), f32),
            vm((4, 2, KX * C, 128), f32),
            vm((4, 2, KX * C, 128), f32),
            vm((3 * GN, 128), f32),
            vm((SHARD, 6 * GN), f32),
            vm((2, 2, C, 4, MODES), bf),
            dma((5,)),
            dma((4,)),
            dma((4,)),
            dma((4, 3)),
            dma((4, 3)),
            dma((2,)),
            dma((2,)),
            dma((3,)),
        ],
        compiler_params=pltpu.CompilerParams(
            collective_id=0, has_side_effects=True, vmem_limit_bytes=56 << 20
        ),
        name="spectral_block",
    )(
        spectra[0].swapaxes(1, 2),
        cotangent[0].swapaxes(1, 2),
        weights,
        jnp.asarray(fb),
        jnp.asarray(fbt),
    )
    out, gin, wg = pl.pallas_call(
        hand_over,
        out_shape=[jax.ShapeDtypeStruct(v.shape, v.dtype) for v in (out, gin, wg)],
        in_specs=[pl.BlockSpec(memory_space=pl.ANY)] * 3,
        out_specs=[pl.BlockSpec(memory_space=pl.ANY)] * 3,
        scratch_shapes=[vm(v.shape, v.dtype) for v in (out, gin, wg)] + [dma((8,)), dma((8,))],
        compiler_params=pltpu.CompilerParams(vmem_limit_bytes=60 << 20),
        name="hand_over",
    )(out, gin, wg)
    return out.swapaxes(1, 2)[None], gin.swapaxes(1, 2)[None], wg


def solution(mesh):
    field = P("ba", None, "gx", None, None)
    return jax.shard_map(
        on_device,
        mesh=mesh,
        in_specs=(field, field, P("gx", None)),
        out_specs=(field, field, P("gx", None)),
        check_vma=False,
    )
```

```python
import functools
import math

import jax
import jax.numpy as jnp
import numpy as np
from jax import lax
from jax.experimental import pallas as pl
from jax.experimental.pallas import tpu as pltpu
from jax.sharding import PartitionSpec as P

C = 20
X = 256
KX = 24
SHARD = 54
MODES = 3456
TILES = MODES // 128
PLANE = 32
COLS = 1152
NT = COLS // 128
GROUP = 8
GN = GROUP * C * C
MESH = pl.DeviceIdType.MESH


def table():
    mode = np.arange(KX)
    wave = np.where(mode < KX // 2, mode, mode - KX)
    phases = wave[:, None] * np.arange(X)[None, :] % X
    angles = phases.astype(np.float32) * np.float32(2.0 * math.pi / X)
    factor = np.float32(1.0 / math.sqrt(X))
    c = np.cos(angles) * factor
    s = np.sin(angles) * factor
    full = np.concatenate([np.concatenate([c, s], 1), np.concatenate([-s, c], 1)], 0)
    return full.astype(jnp.bfloat16).astype(np.float32)


@functools.cache
def constants():
    f = table().reshape(2, 3, GROUP, 2, 2, PLANE, 4)
    f = f.transpose(4, 1, 0, 2, 5, 3, 6)
    fb = np.zeros((2, 2, 48, PLANE, 2, 8), np.float32)
    for z in range(2):
        rows = f[z].reshape(48, PLANE, 8)
        fb[z, 0, :, :, z] = rows
        fb[z, 1, :, :, 1 - z] = rows
    fb = fb.reshape(2, 96, 512)
    bf = lambda a: a.astype(jnp.bfloat16)
    return bf(fb), bf(fb.transpose(0, 2, 1))


def spot(c):
    return 54 * c // 128, 54 * c % 128


def kernel(
    x_hbm, ct_hbm, w_hbm, fb_hbm, fbt_hbm,
    out_hbm, gin_hbm, wg_hbm,
    xb, xs, w, fb, fbt, sbuf, rbuf, zs, zr, coef, vt, vp, vq, wt, mt, ga, gb, wgt, wg, ob,
    load_sem, ssem, rsem, zssem, zrsem, bssem, brsem, out_sem,
):
    me = lax.axis_index("gx")
    ba = lax.axis_index("ba")
    z = me // PLANE
    q = me % PLANE
    qx, qy, qc = q // 8, q // 2 % 4, q % 2

    def peer(j):
        j = 32 - j
        i = j // 2
        return (qx + i) % 4 * 8 + (qy + i // 4 + i) % 4 * 2 + (qc + j) % 2

    def load(i, src, dst):
        copy = pltpu.make_async_copy(src, dst, load_sem.at[i])
        copy.start()
        return copy

    loads = [
        load(0, x_hbm, xb.at[0]),
        load(1, ct_hbm, xb.at[1]),
        load(2, fb_hbm, fb),
        load(3, w_hbm, w),
        load(4, fbt_hbm, fbt),
    ]

    bar = pltpu.get_barrier_semaphore()

    def greet(j, carry):
        pl.semaphore_signal(bar, inc=1, device_id=(z * PLANE + peer(j), ba), device_id_type=MESH)
        return carry

    lax.fori_loop(1, PLANE, greet, 0)
    zpeer = ((1 - z) * PLANE + q, ba)
    pl.semaphore_signal(bar, inc=1, device_id=zpeer, device_id_type=MESH)
    for d in range(1, 4):
        pl.semaphore_signal(bar, inc=1, device_id=(me, (ba + d) % 4), device_id_type=MESH)

    lane = lax.broadcasted_iota(jnp.int32, (8, 128), 1)
    lane16 = lax.broadcasted_iota(jnp.int16, (16, 128), 1)

    def rows8(which, c, cols):
        return jnp.concatenate(
            [xb[which, p, c, :, cols].astype(jnp.float32) for p in range(2)], axis=0
        )

    def arrange(which):
        def tile(t, carry):
            def cols(u):
                return pl.ds(pl.multiple_of(jnp.minimum(u, TILES - 1) * 128, 128), 128)

            for c in range(C):
                low = rows8(which, c, cols(t))
                high = jnp.where(
                    lane >= 64, rows8(which, c, cols(t + 13)), rows8(which, c, cols(t + 14))
                )
                both = jnp.concatenate([low, pltpu.roll(high, 64, 1)], axis=0)
                xs[t, 16 * c : 16 * c + 16, :] = both.astype(jnp.bfloat16)
            return carry

        lax.fori_loop(0, 14, tile, 0)

    def pack(dest, store):
        lane0 = 54 * dest
        t0 = lane0 // 128
        amt = lane0 % 128
        t1 = jnp.minimum(t0 + 1, 13)
        mask = lane16 >= amt.astype(jnp.int16)
        merged = jnp.concatenate(
            [
                jnp.where(mask, xs[t0, 16 * c : 16 * c + 16, :], xs[t1, 16 * c : 16 * c + 16, :])
                for c in range(C)
            ],
            axis=0,
        )
        merged = pltpu.roll(merged, (128 - amt) % 128, 1)
        tiles = [None] * NT
        for c in range(C):
            T, pos = spot(c)
            v = merged[16 * c : 16 * c + 16]
            if pos:
                v = pltpu.roll(v, pos, 1)
            tiles[T] = v if pos == 0 else jnp.where(lane16 >= pos, v, tiles[T])
            if pos + 54 > 128:
                tiles[T + 1] = v
        for T in range(NT):
            store(T, tiles[T])

    def send(phase, dest):
        pltpu.make_async_remote_copy(
            src_ref=sbuf.at[phase, dest],
            dst_ref=rbuf.at[phase, q],
            send_sem=ssem.at[phase],
            recv_sem=rsem.at[phase],
            device_id=(z * PLANE + dest, ba),
            device_id_type=MESH,
        ).start()

    def received(phase):
        part = rbuf.at[phase, pl.ds(0, PLANE - 1)]
        pltpu.make_async_copy(part, part, rsem.at[phase]).wait()

    def scatter(phase):
        def own(T, value):
            rbuf[phase, q, :, T * 128 : T * 128 + 128] = value

        pack(q, own)

        def step(j, carry):
            dest = peer(j)

            def put(T, value):
                sbuf[phase, dest, :, T * 128 : T * 128 + 128] = value

            pack(dest, put)
            send(phase, dest)
            return carry

        lax.fori_loop(1, PLANE, step, 0)

    def swap(slot, g):
        part = (slot, pl.ds(16 * g, 16))
        copy = pltpu.make_async_remote_copy(
            src_ref=zs.at[part], dst_ref=zr.at[part], send_sem=zssem.at[slot, g],
            recv_sem=zrsem.at[slot, g], device_id=zpeer, device_id_type=MESH,
        )
        copy.start()
        return copy

    def transform(phase):
        rows = rbuf[phase].reshape(512, COLS)
        part = jnp.dot(fb[z, 48:96], rows, preferred_element_type=jnp.float32)
        zs[phase] = part.astype(jnp.bfloat16)
        copies = [swap(phase, g) for g in range(3)]
        swaps.extend(copies)
        mine = jnp.dot(fb[z, 0:48], rows, preferred_element_type=jnp.float32)
        return copies, mine

    def turn(phase, copies, mine):
        for g in range(3):
            copies[g].wait_recv()
            got = zr[phase, 16 * g : 16 * g + 16].astype(jnp.float32)
            full = (mine[16 * g : 16 * g + 16] + got).astype(jnp.bfloat16).astype(jnp.float32)
            tiles = [full[:, T * 128 : T * 128 + 128] for T in range(NT)]
            for c in range(C):
                T, pos = spot(c)
                halves = []
                for p in range(2):
                    v = tiles[T][8 * p : 8 * p + 8]
                    if pos + 54 > 128:
                        v = jnp.where(lane >= pos, v, tiles[T + 1][8 * p : 8 * p + 8])
                    shift = (128 + 64 * p - pos) % 128
                    halves.append(pltpu.roll(v, shift, 1) if shift else v)
                v = jnp.where(lane < 64, halves[0], halves[1])
                turned = pltpu.roll(v, 64, 1)
                rows = pl.ds(8 * g * C + c, 8, stride=C)
                vt[rows, :] = v
                if phase == 0:
                    vp[rows, :] = jnp.where(lane < 64, v, -v)
                    vq[rows, :] = turned
                else:
                    vp[rows, :] = v
                    vq[rows, :] = jnp.where(lane < 64, turned, -turned)
        coef[phase, ba] = vt[...].astype(jnp.bfloat16)

    def gather(phase):
        for d in range(1, 4):
            pltpu.make_async_remote_copy(
                src_ref=coef.at[phase, ba], dst_ref=coef.at[phase, ba],
                send_sem=bssem.at[phase], recv_sem=brsem.at[phase],
                device_id=(me, (ba + d) % 4), device_id_type=MESH,
            ).start()

    def gathered(phase):
        part = coef.at[phase, pl.ds(0, 3)]
        pltpu.make_async_copy(part, part, brsem.at[phase]).wait()
        pltpu.make_async_copy(part, part, bssem.at[phase]).wait()

    def turn_weights():
        r = lax.broadcasted_iota(jnp.int32, (128, 128), 0)
        eye = (r == lax.broadcasted_iota(jnp.int32, (128, 128), 1)).astype(jnp.bfloat16)
        zero = jnp.zeros((10, 128), jnp.float32)

        def one(j, carry):
            n0 = pl.multiple_of(j * 128, 128)
            wr = w[:, pl.ds(n0, 128)].astype(jnp.float32)
            wi = w[:, pl.ds(pl.multiple_of(n0 + 3 * GN, 128), 128)].astype(jnp.float32)
            both = jnp.concatenate([wr, zero, wi, zero], axis=0).astype(jnp.bfloat16)
            wt[pl.ds(n0, 128), :] = lax.dot_general(
                eye, both, (((1,), (1,)), ((), ())), preferred_element_type=jnp.float32
            )
            return carry

        lax.fori_loop(0, 3 * GN // 128, one, 0, unroll=5)

    def mix(phase, slot):
        low = lax.broadcasted_iota(jnp.int32, (C, 128), 1) < 64
        for g in range(3):

            def one(kk, carry):
                k = 8 * g + kk
                base = pl.multiple_of(k * (C * C), 8)
                first = second = jnp.zeros((C, 128), jnp.float32)
                for j in range(C):
                    if phase == 0:
                        rows = wt[pl.ds(base + C * j, C), :]
                    else:
                        rows = wt[pl.ds(base + j, C, stride=C), :]
                    first = first + vp[pl.ds(k * C + j, 1), :] * rows
                    second = second + vq[pl.ds(k * C + j, 1), :] * rows
                first = first + pltpu.roll(first, 64, 1)
                second = second + pltpu.roll(second, 64, 1)
                mt[pl.ds(pl.multiple_of(24 * k, 8), C), :] = jnp.where(low, first, second)
                return carry

            lax.fori_loop(0, 8, one, 0)
            halves = [[None] * NT, [None] * NT]
            for c in range(C):
                T, pos = spot(c)
                v = mt[pl.ds(8 * g * 24 + c, 8, stride=24), :]
                for p in range(2):
                    shift = (pos + 64 * p) % 128
                    u = pltpu.roll(v, shift, 1) if shift else v
                    tiles = halves[p]
                    tiles[T] = u if pos == 0 else jnp.where(lane >= pos, u, tiles[T])
                    if pos + 54 > 128:
                        tiles[T + 1] = u
            for T in range(NT):
                both = jnp.concatenate([halves[0][T], halves[1][T]], axis=0)
                zs[slot, 16 * g : 16 * g + 16, T * 128 : T * 128 + 128] = both.astype(jnp.bfloat16)
            swaps.append(swap(slot, g))
        return swaps[-3:]

    def invert(phase, slot, copies):
        for copy in copies:
            copy.wait_recv()
        modes = jnp.concatenate([zs[slot], zr[slot]], axis=0)
        step = 128
        for b in range(512 // step):
            rows = jnp.dot(
                fbt[z, b * step : b * step + step, :], modes, preferred_element_type=jnp.float32
            )
            first = b * step // 16
            sbuf[phase, first : first + step // 16] = rows.astype(jnp.bfloat16).reshape(
                step // 16, 16, COLS
            )
        rbuf[phase, q] = sbuf[phase, q]

        def one(j, carry):
            send(phase, peer(j))
            return carry

        lax.fori_loop(1, PLANE, one, 0)

    def unpack(phase, slot, dst):
        def one(source, carry):
            lane0 = 54 * source
            t0 = lane0 // 128
            amt = lane0 % 128
            mask = lane16 >= amt.astype(jnp.int16)
            tiles = [rbuf[phase, source, :, T * 128 : T * 128 + 128] for T in range(NT)]
            pieces = []
            for c in range(C):
                T, pos = spot(c)
                v = tiles[T]
                if pos + 54 > 128:
                    v = jnp.where(lane16 >= pos, v, tiles[T + 1])
                pieces.append(pltpu.roll(v, 128 - pos, 1) if pos else v)
            merged = pltpu.roll(jnp.concatenate(pieces, axis=0), amt, 1)
            for c in range(C):
                rows = slice(16 * c, 16 * c + 16)
                v = merged[rows]
                xs[t0, rows, :] = jnp.where(mask, v, xs[t0, rows, :])
                xs[t0 + 1, rows, :] = v
            return carry

        lax.fori_loop(0, PLANE, one, 0, unroll=4)

        def put(t, c, value):
            cols = pl.ds(pl.multiple_of(t * 128, 128), 128)
            for p in range(2):
                ob[slot, p, c, :, cols] = value[4 * p : 4 * p + 4].astype(jnp.bfloat16)

        def tile(t, carry):
            for c in range(C):
                rows = slice(16 * c, 16 * c + 16)
                here = xs[t, rows, :].astype(jnp.float32)
                after = xs[t + 1, rows, :].astype(jnp.float32)
                put(t, c, here[0:8])
                high = jnp.where(lane >= 64, here[8:16], after[8:16])
                put(t + 14, c, pltpu.roll(high, 64, 1))
            return carry

        lax.fori_loop(0, 13, tile, 0)
        for c in range(C):
            rows = slice(16 * c, 16 * c + 16)
            high = pltpu.roll(xs[0, rows, :].astype(jnp.float32)[8:16], 64, 1)
            low = xs[13, rows, :].astype(jnp.float32)[0:8]
            put(13, c, jnp.where(lane < 64, low, high))
        copy = pltpu.make_async_copy(ob.at[slot], dst, out_sem.at[slot])
        copy.start()
        return copy

    def outer():
        low = lax.broadcasted_iota(jnp.int32, (24 * C, 128), 1) < 64
        for s in range(4):
            a = coef[0, s].astype(jnp.float32)
            turned = pltpu.roll(a, 64, 1)
            ga[s, 0] = jnp.where(low, a, turned)
            ga[s, 1] = jnp.where(low, turned, a)
            b = coef[1, s].astype(jnp.float32)
            turned = pltpu.roll(b, 64, 1)
            gb[s, 0] = b
            gb[s, 1] = jnp.where(low, turned, -turned)

        def one(k, carry):
            base = pl.multiple_of(k * (C * C), 8)
            right = [[gb[s, u, pl.ds(k * C, C), :] for u in range(2)] for s in range(4)]
            for i in range(C):
                total = None
                for s in range(4):
                    for u in range(2):
                        term = ga[s, u, pl.ds(k * C + i, 1), :] * right[s][u]
                        total = term if total is None else total + term
                wgt[pl.ds(base + C * i, C), :] = total
            return carry

        lax.fori_loop(0, KX, one, 0)

        def flip(j, carry):
            n0 = pl.multiple_of(j * 128, 128)
            both = wgt[pl.ds(n0, 128), :].T
            wg[:, pl.ds(n0, 128)] = both[0:54]
            wg[:, pl.ds(pl.multiple_of(n0 + 3 * GN, 128), 128)] = both[64:118]
            return carry

        lax.fori_loop(0, 3 * GN // 128, flip, 0, unroll=5)
        copy = pltpu.make_async_copy(wg, wg_hbm, out_sem.at[2])
        copy.start()
        return copy

    swaps = []
    loads[0].wait()
    arrange(0)
    pl.semaphore_wait(bar, PLANE - 1 + 1 + 3)
    scatter(0)
    loads[1].wait()
    arrange(1)
    scatter(1)
    for copy in loads[2:]:
        copy.wait()
    turn_weights()
    received(0)
    turn(0, *transform(0))
    back = mix(0, 2)
    received(1)
    front = transform(1)
    invert(2, 2, back)
    gather(0)
    turn(1, *front)
    back = mix(1, 3)
    gather(1)
    invert(3, 3, back)
    received(2)
    done = [unpack(2, 0, out_hbm)]
    gathered(0)
    gathered(1)
    done.append(outer())
    received(3)
    done.append(unpack(3, 1, gin_hbm))
    for copy in swaps:
        copy.wait_send()
    for phase in range(4):
        part = sbuf.at[phase, pl.ds(0, PLANE - 1)]
        pltpu.make_async_copy(part, part, ssem.at[phase]).wait()
    for copy in done:
        copy.wait()


def hand_over(a, b, c, to_a, to_b, to_c, va, vb, vc, sem, sem_out):
    parts = []
    for first, rows in ((0, 16), (16, 16), (32, 16), (48, 6)):
        parts.append((c, vc, to_c, (pl.ds(first, rows),)))
    for src, mid, dst in ((a, va, to_a), (b, vb, to_b)):
        for p in range(2):
            parts.append((src, mid, dst, (p,)))
    loads = []
    for n, (src, mid, dst, part) in enumerate(parts):
        loads.append(pltpu.make_async_copy(src.at[part], mid.at[part], sem.at[n]))
        loads[-1].start()
    stores = []
    for n, (src, mid, dst, part) in enumerate(parts):
        loads[n].wait()
        stores.append(pltpu.make_async_copy(mid.at[part], dst.at[part], sem_out.at[n]))
        stores[-1].start()
    for copy in stores:
        copy.wait()


def on_device(spectra, cotangent, weights):
    fb, fbt = constants()
    bf, f32 = jnp.bfloat16, jnp.float32
    vm = pltpu.VMEM
    dma = pltpu.SemaphoreType.DMA
    out, gin, wg = pl.pallas_call(
        kernel,
        out_shape=[
            jax.ShapeDtypeStruct((2, C, 4, MODES), bf),
            jax.ShapeDtypeStruct((2, C, 4, MODES), bf),
            jax.ShapeDtypeStruct((SHARD, 6 * GN), f32),
        ],
        in_specs=[pl.BlockSpec(memory_space=pl.ANY)] * 5,
        out_specs=[pl.BlockSpec(memory_space=pl.ANY)] * 3,
        scratch_shapes=[
            vm((2, 2, C, 4, MODES), bf),
            vm((15, 16 * C, 128), bf),
            vm((SHARD, 6 * GN), bf),
            vm((2, 96, 512), bf),
            vm((2, 512, 96), bf),
            vm((4, PLANE, 16, COLS), bf),
            vm((4, PLANE, 16, COLS), bf),
            vm((4, 48, COLS), bf),
            vm((4, 48, COLS), bf),
            vm((2, 4, KX * C, 128), bf),
            vm((KX * C, 128), f32),
            vm((KX * C, 128), f32),
            vm((KX * C, 128), f32),
            vm((3 * GN, 128), f32),
            vm((KX * 24, 128), f32),
            vm((4, 2, KX * C, 128), f32),
            vm((4, 2, KX * C, 128), f32),
            vm((3 * GN, 128), f32),
            vm((SHARD, 6 * GN), f32),
            vm((2, 2, C, 4, MODES), bf),
            dma((5,)),
            dma((4,)),
            dma((4,)),
            dma((4, 3)),
            dma((4, 3)),
            dma((2,)),
            dma((2,)),
            dma((3,)),
        ],
        compiler_params=pltpu.CompilerParams(
            collective_id=0, has_side_effects=True, vmem_limit_bytes=56 << 20
        ),
        name="spectral_block",
    )(
        spectra[0].swapaxes(1, 2),
        cotangent[0].swapaxes(1, 2),
        weights,
        jnp.asarray(fb),
        jnp.asarray(fbt),
    )
    out, gin, wg = pl.pallas_call(
        hand_over,
        out_shape=[jax.ShapeDtypeStruct(v.shape, v.dtype) for v in (out, gin, wg)],
        in_specs=[pl.BlockSpec(memory_space=pl.ANY)] * 3,
        out_specs=[pl.BlockSpec(memory_space=pl.ANY)] * 3,
        scratch_shapes=[vm(v.shape, v.dtype) for v in (out, gin, wg)] + [dma((8,)), dma((8,))],
        compiler_params=pltpu.CompilerParams(vmem_limit_bytes=60 << 20),
        name="hand_over",
    )(out, gin, wg)
    return out.swapaxes(1, 2)[None], gin.swapaxes(1, 2)[None], wg


def solution(mesh):
    field = P("ba", None, "gx", None, None)
    return jax.shard_map(
        on_device,
        mesh=mesh,
        in_specs=(field, field, P("gx", None)),
        out_specs=(field, field, P("gx", None)),
        check_vma=False,
    )
```
